32 devices in a mesh: elem: 4 (over z), tm: 8 (over y, x, core).
Axes of the slice: x: 2, y: 2, z: 4, core: 2. Of those that a mesh axis runs over, the one named last changes fastest.
Arguments:
- samples: bfloat16 [6144, 2048], P('tm', 'elem'), may hold values from -160 to 160
- taps_weight: bfloat16 [16, 2048, 512], P(None, 'elem'), may hold values from -0.046875 to 0.046875
- retain: float32 [6144], P('tm')
Outputs:
- whitened: float32 [512, 6144], P('elem', 'tm')
The draws below stay inside these ranges and needn't reach their ends.
All inputs are finite; a program needn't handle non-finite values.
Results may differ from the reference program's by a relative error of at most 0.0003.
Values may be sent and summed in bfloat16 or wider, within the bound.
A program may use at most 192 MiB of HBM per device.

```python
import jax
import jax.numpy as jnp
from jax import lax

ELEMENTS = 2048
BEAMS = 512
TAPS = 16
TM_DEV = 768
SAMPLES = 6144
N_TM = 8


def draw_samples(key, part):
    keys = jax.random.split(jax.random.fold_in(key, 11), 6)
    power_matrix = jnp.arange(SAMPLES, dtype=jnp.int32)[:, None]
    envelope = jnp.exp(jnp.log(3.0) * power_matrix.astype(jnp.float32) / SAMPLES)
    noise = jnp.clip(jax.random.normal(keys[0], (SAMPLES, ELEMENTS), jnp.float32), -5.0, 5.0)
    element_gain = jnp.exp(jax.random.uniform(keys[1], (1, ELEMENTS), jnp.float32, jnp.log(0.5), jnp.log(2.0)))
    sources = jnp.clip(jax.random.normal(keys[2], (SAMPLES, 4), jnp.float32), -5.0, 5.0)
    steering = jnp.clip(jax.random.normal(keys[3], (4, ELEMENTS), jnp.float32), -3.0, 3.0)
    onsets = jax.random.randint(keys[4], (4,), 0, SAMPLES)
    spans = jax.random.randint(keys[5], (4,), SAMPLES // 8, SAMPLES // 2)
    active = jnp.logical_and(power_matrix >= onsets[None, :], power_matrix < onsets[None, :] + spans[None, :]).astype(jnp.float32)
    result = noise * element_gain * envelope
    for emitter_number in range(4):
        result = result + (2.0 * active[:, emitter_number] * sources[:, emitter_number])[:, None] * steering[emitter_number][None, :]
    return result.astype(jnp.bfloat16)


def draw_retain(key, part):
    keys = jax.random.split(jax.random.fold_in(key, 23), 2)
    spread = jax.random.uniform(keys[0], (SAMPLES,), jnp.float32, 0.2, 1.8)
    retained_readings = jnp.exp(-spread / SAMPLES)
    receiver_locations = jax.random.randint(keys[1], (3,), 0, SAMPLES)
    power_matrix = jnp.arange(SAMPLES, dtype=jnp.int32)
    pulse_clusters = jnp.sum((power_matrix[:, None] == receiver_locations[None, :]).astype(jnp.int32), axis=1) > 0
    return jnp.where(pulse_clusters, 0.7, retained_readings).astype(jnp.float32)


def strengthened(drawn, key, source, target, shards_of, factor):
    def block_of(axis_at):
        return (jnp.arange(drawn.shape[axis_at]) // (drawn.shape[axis_at] // shards_of)).reshape((-1,) + (1,) * (drawn.ndim - 1 - axis_at))

    near = jax.random.permutation(key, shards_of)[block_of(target)]
    far = (block_of(target) + shards_of // 2) % shards_of
    return jnp.where((block_of(source) == near) | (block_of(source) == far), factor * drawn, drawn)


def block_levels(rng, shape, pieces, least, high):
    def one(position, shards_of):
        heights = jax.random.uniform(jax.random.fold_in(jax.random.fold_in(rng, 6), position), (shards_of,), jnp.float32, least / len(pieces), high / len(pieces))
        return jnp.repeat(jnp.exp(heights), shape[position] // shards_of).reshape((-1,) + (1,) * (len(shape) - position - 1))

    factor_of = one(*pieces[0])
    for cut in pieces[1:]:
        factor_of = factor_of * one(*cut)
    return factor_of


def gaussian_with(key, extent, scale, most, pieces, heavy, kind=jnp.bfloat16):
    values = scale * jax.random.normal(key, extent, jnp.float32)
    if pieces:
        values = values * block_levels(key, extent, pieces, -0.22, 0.18)
    return jnp.clip(strengthened(values, jax.random.fold_in(key, 3), *heavy), -most, most).astype(kind)


def setup_inputs(seed: int = 0) -> dict:
    seeds = jax.random.split(jax.random.key(seed), 4)
    samples = draw_samples(jax.random.fold_in(seeds[3], 71), 0)
    taps_weight = gaussian_with(seeds[1], (TAPS, ELEMENTS, BEAMS), (TAPS * ELEMENTS) ** -0.5, 0.046875, ((1, 4),), (1, 2, 4, 2.0))
    retain = draw_retain(jax.random.fold_in(seeds[3], 71), 0)
    return {"samples": samples, "taps_weight": taps_weight, "retain": retain}


loading_level = 0.1

def reference(samples, taps_weight, retain):
    filters = taps_weight.astype(jnp.float32).reshape(TAPS * ELEMENTS, BEAMS)
    padded = jnp.concatenate([jnp.zeros((TAPS - 1, ELEMENTS), jnp.float32), samples.astype(jnp.float32)], 0)
    unit_matrix = jnp.eye(BEAMS, dtype=jnp.float32)

    def advance(carry, block_index):
        gram_sum, count_sum = carry
        first_row = block_index * TM_DEV
        window_rows = lax.dynamic_slice_in_dim(padded, first_row, TM_DEV + TAPS - 1, 0)
        windowed = jnp.concatenate([window_rows[TAPS - 1 - filter_tap_index:TAPS - 1 - filter_tap_index + TM_DEV] for filter_tap_index in range(TAPS)], 1)
        beam_rows = jnp.dot(windowed, filters, precision=lax.Precision.HIGHEST)
        log_retain = jnp.log(lax.dynamic_slice_in_dim(retain, first_row, TM_DEV, 0))
        log_total = jnp.sum(log_retain)
        row_weight = jnp.exp(log_total - jnp.cumsum(log_retain))
        factor = jnp.exp(log_total)
        gram_block = jnp.dot((beam_rows * row_weight[:, None]).T, beam_rows, precision=lax.Precision.HIGHEST)
        gram_sum = factor * gram_sum + gram_block
        count_sum = factor * count_sum + jnp.sum(row_weight)
        covariance_estimate = gram_sum / count_sum + loading_level * unit_matrix
        lower_factor = jnp.linalg.cholesky(covariance_estimate)
        inverse_lower = jax.scipy.linalg.solve_triangular(lower_factor, unit_matrix, lower=True)
        whitened_block = lax.dot_general(inverse_lower, beam_rows, (((1,), (1,)), ((), ())), precision=lax.Precision.HIGHEST)
        return ((gram_sum, count_sum), whitened_block)
    initial = (jnp.zeros((BEAMS, BEAMS), jnp.float32), jnp.zeros((), jnp.float32))
    final_state, blocks = lax.scan(advance, initial, jnp.arange(N_TM, dtype=jnp.int32))
    return jnp.transpose(blocks, (1, 0, 2)).reshape(BEAMS, SAMPLES)
```

```python
import jax
import jax.numpy as jnp
from jax import lax
from jax.experimental import pallas as pl
from jax.experimental.pallas import tpu as pltpu
from jax.sharding import PartitionSpec as P

loading_level = 0.1
BLOCK = 128
PIVOTS = 4
LANES = 128


def shifted(array, axis, by):
    size = lax.axis_size(axis)
    pairs = [(i, i + by) for i in range(size) if 0 <= i + by < size]
    return lax.ppermute(array, axis, pairs)


def eliminate(square):
    lane = lax.broadcasted_iota(jnp.int32, (8, LANES), 1)
    groups = [square[8 * g : 8 * g + 8] for g in range(BLOCK // 8)]
    finished = []
    for first in range(0, BLOCK, PIVOTS):
        home = first // 8
        live = range(home, BLOCK // 8)
        inside = (lane >= first) & (lane < first + PIVOTS)
        columns = {
            g: [
                jnp.broadcast_to(groups[g][:, first + j : first + j + 1], (8, LANES))
                for j in range(PIVOTS)
            ]
            for g in live
        }
        offset = first % 8
        pivot = [
            [
                jnp.broadcast_to(columns[home][j][offset + i : offset + i + 1], (8, LANES))
                for j in range(i + 1)
            ]
            for i in range(PIVOTS)
        ]
        rows = [
            jnp.where(
                inside,
                (lane == first + j).astype(jnp.float32),
                jnp.broadcast_to(groups[home][offset + j : offset + j + 1], (8, LANES)),
            )
            for j in range(PIVOTS)
        ]
        inverse, ratio = [], {}
        for j in range(PIVOTS):
            inverse.append(1.0 / pivot[j][j])
            for i in range(j + 1, PIVOTS):
                ratio[i, j] = pivot[i][j] * inverse[j]
            for i in range(j + 1, PIVOTS):
                rows[i] = rows[i] - ratio[i, j] * rows[j]
                for m in range(j + 1, i + 1):
                    pivot[i][m] = pivot[i][m] - ratio[i, j] * pivot[m][j]
        for j in range(PIVOTS):
            finished.append((rows[j] * lax.rsqrt(pivot[j][j]))[:1])
        solved = [rows[j] * inverse[j] for j in range(PIVOTS)]
        for j in reversed(range(PIVOTS)):
            for i in range(j):
                solved[i] = solved[i] - ratio[j, i] * solved[j]
        for g in live:
            change = columns[g][0] * solved[0]
            for j in range(1, PIVOTS):
                change = change + columns[g][j] * solved[j]
            groups[g] = jnp.where(inside, 0.0, groups[g]) - change
    whole = jnp.concatenate(finished, 0)
    row = lax.broadcasted_iota(jnp.int32, (BLOCK, BLOCK), 0)
    column = lax.broadcasted_iota(jnp.int32, (BLOCK, BLOCK), 1)
    return jnp.where(column <= row, whole, 0.0)


def inverse_factor_kernel(covariance_ref, out_ref, work):
    size = covariance_ref.shape[0]
    work[...] = covariance_ref[...]

    @pl.loop(0, size // BLOCK)
    def _(block):
        start = pl.multiple_of(block * BLOCK, BLOCK)
        corner = eliminate(work[pl.ds(start, BLOCK), pl.ds(start, BLOCK)])
        wide_row = lax.broadcasted_iota(jnp.int32, (BLOCK, size), 0)
        wide_column = lax.broadcasted_iota(jnp.int32, (BLOCK, size), 1)
        here = (wide_column >= start) & (wide_column < start + BLOCK)
        strip = jnp.where(
            here, (wide_column == start + wide_row).astype(jnp.float32), work[pl.ds(start, BLOCK), :]
        )
        strip = jnp.dot(
            corner, strip, precision=lax.Precision.HIGHEST, preferred_element_type=jnp.float32
        )
        later = jnp.where(wide_column >= start + BLOCK, strip, 0.0)
        change = lax.dot_general(
            later,
            strip,
            (((0,), (0,)), ((), ())),
            precision=lax.Precision.HIGHEST,
            preferred_element_type=jnp.float32,
        )
        row = lax.broadcasted_iota(jnp.int32, (size, size), 0)
        column = lax.broadcasted_iota(jnp.int32, (size, size), 1)
        cleared = (row >= start + BLOCK) & (column >= start) & (column < start + BLOCK)
        work[...] = jnp.where(cleared, 0.0, work[...]) - change
        out_ref[pl.ds(start, BLOCK), :] = jnp.where(
            wide_column <= start + wide_row, strip, 0.0
        )


def inverse_factor(covariance):
    size = covariance.shape[0]
    return pl.pallas_call(
        inverse_factor_kernel,
        out_shape=jax.ShapeDtypeStruct((size, size), jnp.float32),
        in_specs=[pl.BlockSpec(memory_space=pltpu.VMEM)],
        out_specs=pl.BlockSpec(memory_space=pltpu.VMEM),
        scratch_shapes=[pltpu.VMEM((size, size), jnp.float32)],
        compiler_params=pltpu.CompilerParams(vmem_limit_bytes=32 * 1024 * 1024),
        cost_estimate=pl.CostEstimate(
            flops=12 * size**3, bytes_accessed=8 * size**2, transcendentals=0
        ),
    )(covariance)


def local(samples, taps_weight, retain):
    row_count = samples.shape[0]
    elem_width = samples.shape[1]
    tap_count = taps_weight.shape[0]
    beam_count = taps_weight.shape[2]
    sample_history = shifted(samples[row_count - (tap_count - 1) :], "tm", 1)
    extended = jnp.concatenate([sample_history, samples], 0)
    windowed = jnp.concatenate(
        [
            extended[
                tap_count - 1 - filter_tap_index : tap_count - 1 - filter_tap_index + row_count
            ]
            for filter_tap_index in range(tap_count)
        ],
        1,
    )
    filters = taps_weight.reshape(tap_count * elem_width, beam_count)
    log_retain = jnp.log(retain)
    log_total = jnp.sum(log_retain)
    row_weight = jnp.exp(log_total - jnp.cumsum(log_retain))
    factor = jnp.exp(log_total)
    mass = jnp.sum(row_weight)
    groups = lax.axis_size("elem")
    mine = lax.axis_index("elem")
    blocks = lax.axis_size("tm")
    block = lax.axis_index("tm")
    columns = beam_count // groups
    beam_rows = lax.psum(jnp.dot(windowed, filters, preferred_element_type=jnp.float32), "elem")
    own_columns = lax.dynamic_slice_in_dim(beam_rows, mine * columns, columns, 1)
    gram_rows = lax.dot_general(
        own_columns * row_weight[:, None],
        beam_rows,
        (((0,), (0,)), ((), ())),
        precision=lax.Precision.HIGHEST,
    )
    scalars = jnp.concatenate(
        [jnp.full((4, beam_count), mass), jnp.full((4, beam_count), factor)], 0
    )
    pieces = lax.all_gather(jnp.concatenate([gram_rows, scalars], 0), "tm")
    total = jnp.zeros((columns, beam_count), jnp.float32)
    count = jnp.zeros((1, beam_count), jnp.float32)
    for position in range(blocks):
        decay = pieces[position, columns + 4 : columns + 5]
        taken = position <= block
        total = jnp.where(taken, total * decay + pieces[position, :columns], total)
        count = jnp.where(taken, count * decay + pieces[position, columns : columns + 1], count)
    diagonal = (
        lax.broadcasted_iota(jnp.int32, (columns, beam_count), 1)
        == lax.broadcasted_iota(jnp.int32, (columns, beam_count), 0) + mine * columns
    )
    covariance_rows = total / count + jnp.where(diagonal, loading_level, 0.0)
    covariance = lax.all_gather(covariance_rows, "elem", tiled=True)
    inverse_lower = inverse_factor(covariance)
    local_rows = lax.dynamic_slice_in_dim(inverse_lower, mine * columns, columns, 0)
    return lax.dot_general(
        local_rows, beam_rows, (((1,), (1,)), ((), ())), precision=lax.Precision.HIGHEST
    )


def solution(mesh):
    placed = (P("tm", "elem"), P(None, "elem", None), P("tm"))
    return jax.shard_map(
        local, mesh=mesh, in_specs=placed, out_specs=P("elem", "tm"), check_vma=False
    )
```

```python
import jax
import jax.numpy as jnp
from jax import lax
from jax.experimental import pallas as pl
from jax.experimental.pallas import tpu as pltpu
from jax.sharding import PartitionSpec as P

loading_level = 0.1
BLOCK = 128
PIVOTS = 4
LANES = 128


def shifted(array, axis, by):
    size = lax.axis_size(axis)
    pairs = [(i, i + by) for i in range(size) if 0 <= i + by < size]
    return lax.ppermute(array, axis, pairs)


def eliminate(square):
    lane = lax.broadcasted_iota(jnp.int32, (8, LANES), 1)
    groups = [square[8 * g : 8 * g + 8] for g in range(BLOCK // 8)]
    finished = []
    for first in range(0, BLOCK, PIVOTS):
        home = first // 8
        live = range(home, BLOCK // 8)
        inside = (lane >= first) & (lane < first + PIVOTS)
        columns = {
            g: [
                jnp.broadcast_to(groups[g][:, first + j : first + j + 1], (8, LANES))
                for j in range(PIVOTS)
            ]
            for g in live
        }
        offset = first % 8
        pivot = [
            [
                jnp.broadcast_to(columns[home][j][offset + i : offset + i + 1], (8, LANES))
                for j in range(i + 1)
            ]
            for i in range(PIVOTS)
        ]
        rows = [
            jnp.where(
                inside,
                (lane == first + j).astype(jnp.float32),
                jnp.broadcast_to(groups[home][offset + j : offset + j + 1], (8, LANES)),
            )
            for j in range(PIVOTS)
        ]
        inverse, ratio = [], {}
        for j in range(PIVOTS):
            inverse.append(1.0 / pivot[j][j])
            for i in range(j + 1, PIVOTS):
                ratio[i, j] = pivot[i][j] * inverse[j]
            for i in range(j + 1, PIVOTS):
                rows[i] = rows[i] - ratio[i, j] * rows[j]
                for m in range(j + 1, i + 1):
                    pivot[i][m] = pivot[i][m] - ratio[i, j] * pivot[m][j]
        for j in range(PIVOTS):
            finished.append((rows[j] * lax.rsqrt(pivot[j][j]))[:1])
        solved = [rows[j] * inverse[j] for j in range(PIVOTS)]
        for j in reversed(range(PIVOTS)):
            for i in range(j):
                solved[i] = solved[i] - ratio[j, i] * solved[j]
        for g in live:
            change = columns[g][0] * solved[0]
            for j in range(1, PIVOTS):
                change = change + columns[g][j] * solved[j]
            groups[g] = jnp.where(inside, 0.0, groups[g]) - change
    whole = jnp.concatenate(finished, 0)
    row = lax.broadcasted_iota(jnp.int32, (BLOCK, BLOCK), 0)
    column = lax.broadcasted_iota(jnp.int32, (BLOCK, BLOCK), 1)
    return jnp.where(column <= row, whole, 0.0)


def inverse_factor_kernel(covariance_ref, out_ref, work):
    size = covariance_ref.shape[0]
    work[...] = covariance_ref[...]

    @pl.loop(0, size // BLOCK)
    def _(block):
        start = pl.multiple_of(block * BLOCK, BLOCK)
        corner = eliminate(work[pl.ds(start, BLOCK), pl.ds(start, BLOCK)])
        wide_row = lax.broadcasted_iota(jnp.int32, (BLOCK, size), 0)
        wide_column = lax.broadcasted_iota(jnp.int32, (BLOCK, size), 1)
        here = (wide_column >= start) & (wide_column < start + BLOCK)
        strip = jnp.where(
            here, (wide_column == start + wide_row).astype(jnp.float32), work[pl.ds(start, BLOCK), :]
        )
        strip = jnp.dot(
            corner, strip, precision=lax.Precision.HIGHEST, preferred_element_type=jnp.float32
        )
        later = jnp.where(wide_column >= start + BLOCK, strip, 0.0)
        change = lax.dot_general(
            later,
            strip,
            (((0,), (0,)), ((), ())),
            precision=lax.Precision.HIGHEST,
            preferred_element_type=jnp.float32,
        )
        row = lax.broadcasted_iota(jnp.int32, (size, size), 0)
        column = lax.broadcasted_iota(jnp.int32, (size, size), 1)
        cleared = (row >= start + BLOCK) & (column >= start) & (column < start + BLOCK)
        work[...] = jnp.where(cleared, 0.0, work[...]) - change
        out_ref[pl.ds(start, BLOCK), :] = jnp.where(
            wide_column <= start + wide_row, strip, 0.0
        )


def inverse_factor(covariance):
    size = covariance.shape[0]
    return pl.pallas_call(
        inverse_factor_kernel,
        out_shape=jax.ShapeDtypeStruct((size, size), jnp.float32),
        in_specs=[pl.BlockSpec(memory_space=pltpu.VMEM)],
        out_specs=pl.BlockSpec(memory_space=pltpu.VMEM),
        scratch_shapes=[pltpu.VMEM((size, size), jnp.float32)],
        compiler_params=pltpu.CompilerParams(vmem_limit_bytes=32 * 1024 * 1024),
        cost_estimate=pl.CostEstimate(
            flops=12 * size**3, bytes_accessed=8 * size**2, transcendentals=0
        ),
    )(covariance)


def local(samples, taps_weight, retain):
    row_count = samples.shape[0]
    elem_width = samples.shape[1]
    tap_count = taps_weight.shape[0]
    beam_count = taps_weight.shape[2]
    sample_history = shifted(samples[row_count - (tap_count - 1) :], "tm", 1)
    extended = jnp.concatenate([sample_history, samples], 0)
    windowed = jnp.concatenate(
        [
            extended[
                tap_count - 1 - filter_tap_index : tap_count - 1 - filter_tap_index + row_count
            ]
            for filter_tap_index in range(tap_count)
        ],
        1,
    )
    filters = taps_weight.reshape(tap_count * elem_width, beam_count)
    log_retain = jnp.log(retain)
    log_total = jnp.sum(log_retain)
    row_weight = jnp.exp(log_total - jnp.cumsum(log_retain))
    factor = jnp.exp(log_total)
    mass = jnp.sum(row_weight)
    groups = lax.axis_size("elem")
    mine = lax.axis_index("elem")
    blocks = lax.axis_size("tm")
    block = lax.axis_index("tm")
    columns = beam_count // groups
    beam_rows = lax.psum(jnp.dot(windowed, filters, preferred_element_type=jnp.float32), "elem")
    weighted = beam_rows * row_weight[:, None]
    strips = [
        lax.dot_general(
            weighted[:, start : start + BLOCK],
            beam_rows[:, start:],
            (((0,), (0,)), ((), ())),
            precision=lax.Precision.HIGHEST,
        )
        for start in range(0, beam_count, BLOCK)
    ]
    packed = jnp.concatenate(strips, 1)
    width = packed.shape[1]
    scalars = jnp.concatenate([jnp.full((4, width), mass), jnp.full((4, width), factor)], 0)
    pieces = lax.all_gather(jnp.concatenate([packed, scalars], 0), "tm")
    total = jnp.zeros((BLOCK, width), jnp.float32)
    count = jnp.zeros((1, width), jnp.float32)
    for position in range(blocks):
        decay = pieces[position, BLOCK + 4 : BLOCK + 5]
        taken = position <= block
        total = jnp.where(taken, total * decay + pieces[position, :BLOCK], total)
        count = jnp.where(taken, count * decay + pieces[position, BLOCK : BLOCK + 1], count)
    estimate = total / count
    upper, at = [], 0
    for start in range(0, beam_count, BLOCK):
        strip = estimate[:, at : at + beam_count - start]
        at += beam_count - start
        upper.append(jnp.pad(strip, ((0, 0), (start, 0))))
    covariance = jnp.concatenate(upper, 0) + loading_level * jnp.eye(beam_count, dtype=jnp.float32)
    inverse_lower = inverse_factor(covariance)
    local_rows = lax.dynamic_slice_in_dim(inverse_lower, mine * columns, columns, 0)
    return lax.dot_general(
        local_rows, beam_rows, (((1,), (1,)), ((), ())), precision=lax.Precision.HIGHEST
    )


def solution(mesh):
    placed = (P("tm", "elem"), P(None, "elem", None), P("tm"))
    return jax.shard_map(
        local, mesh=mesh, in_specs=placed, out_specs=P("elem", "tm"), check_vma=False
    )
```

```python
import functools

import jax
import jax.numpy as jnp
from jax import lax
from jax.experimental import pallas as pl
from jax.experimental.pallas import tpu as pltpu
from jax.sharding import PartitionSpec as P

loading_level = 0.1
BLOCK = 128
PIVOTS = 4
LANES = 128
CHUNK = 64
LAG = 3
MESH = pl.DeviceIdType.MESH


def shifted(array, axis, by):
    size = lax.axis_size(axis)
    pairs = [(i, i + by) for i in range(size) if 0 <= i + by < size]
    return lax.ppermute(array, axis, pairs)


def eliminate(square):
    lane = lax.broadcasted_iota(jnp.int32, (8, LANES), 1)
    groups = [square[8 * g : 8 * g + 8] for g in range(BLOCK // 8)]
    finished = []
    for first in range(0, BLOCK, PIVOTS):
        home = first // 8
        live = range(home, BLOCK // 8)
        inside = (lane >= first) & (lane < first + PIVOTS)
        columns = {
            g: [
                jnp.broadcast_to(groups[g][:, first + j : first + j + 1], (8, LANES))
                for j in range(PIVOTS)
            ]
            for g in live
        }
        offset = first % 8
        pivot = [
            [
                jnp.broadcast_to(columns[home][j][offset + i : offset + i + 1], (8, LANES))
                for j in range(i + 1)
            ]
            for i in range(PIVOTS)
        ]
        rows = [
            jnp.where(
                inside,
                (lane == first + j).astype(jnp.float32),
                jnp.broadcast_to(groups[home][offset + j : offset + j + 1], (8, LANES)),
            )
            for j in range(PIVOTS)
        ]
        inverse, ratio = [], {}
        for j in range(PIVOTS):
            inverse.append(1.0 / pivot[j][j])
            for i in range(j + 1, PIVOTS):
                ratio[i, j] = pivot[i][j] * inverse[j]
            for i in range(j + 1, PIVOTS):
                rows[i] = rows[i] - ratio[i, j] * rows[j]
                for m in range(j + 1, i + 1):
                    pivot[i][m] = pivot[i][m] - ratio[i, j] * pivot[m][j]
        for j in range(PIVOTS):
            finished.append((rows[j] * lax.rsqrt(pivot[j][j]))[:1])
        solved = [rows[j] * inverse[j] for j in range(PIVOTS)]
        for j in reversed(range(PIVOTS)):
            for i in range(j):
                solved[i] = solved[i] - ratio[j, i] * solved[j]
        for g in live:
            change = columns[g][0] * solved[0]
            for j in range(1, PIVOTS):
                change = change + columns[g][j] * solved[j]
            groups[g] = jnp.where(inside, 0.0, groups[g]) - change
    whole = jnp.concatenate(finished, 0)
    row = lax.broadcasted_iota(jnp.int32, (BLOCK, BLOCK), 0)
    column = lax.broadcasted_iota(jnp.int32, (BLOCK, BLOCK), 1)
    return jnp.where(column <= row, whole, 0.0)


def inverse_factor_kernel(covariance_ref, out_ref, work):
    size = covariance_ref.shape[0]
    work[...] = covariance_ref[...]

    @pl.loop(0, size // BLOCK)
    def _(block):
        start = pl.multiple_of(block * BLOCK, BLOCK)
        corner = eliminate(work[pl.ds(start, BLOCK), pl.ds(start, BLOCK)])
        wide_row = lax.broadcasted_iota(jnp.int32, (BLOCK, size), 0)
        wide_column = lax.broadcasted_iota(jnp.int32, (BLOCK, size), 1)
        here = (wide_column >= start) & (wide_column < start + BLOCK)
        strip = jnp.where(
            here, (wide_column == start + wide_row).astype(jnp.float32), work[pl.ds(start, BLOCK), :]
        )
        strip = jnp.dot(
            corner, strip, precision=lax.Precision.HIGHEST, preferred_element_type=jnp.float32
        )
        later = jnp.where(wide_column >= start + BLOCK, strip, 0.0)
        change = lax.dot_general(
            later,
            strip,
            (((0,), (0,)), ((), ())),
            precision=lax.Precision.HIGHEST,
            preferred_element_type=jnp.float32,
        )
        row = lax.broadcasted_iota(jnp.int32, (size, size), 0)
        column = lax.broadcasted_iota(jnp.int32, (size, size), 1)
        cleared = (row >= start + BLOCK) & (column >= start) & (column < start + BLOCK)
        work[...] = jnp.where(cleared, 0.0, work[...]) - change
        out_ref[pl.ds(start, BLOCK), :] = jnp.where(
            wide_column <= start + wide_row, strip, 0.0
        )


def inverse_factor(covariance):
    size = covariance.shape[0]
    return pl.pallas_call(
        inverse_factor_kernel,
        out_shape=jax.ShapeDtypeStruct((size, size), jnp.float32),
        in_specs=[pl.BlockSpec(memory_space=pltpu.VMEM)],
        out_specs=pl.BlockSpec(memory_space=pltpu.VMEM),
        scratch_shapes=[pltpu.VMEM((size, size), jnp.float32)],
        compiler_params=pltpu.CompilerParams(vmem_limit_bytes=32 * 1024 * 1024),
        cost_estimate=pl.CostEstimate(
            flops=12 * size**3, bytes_accessed=8 * size**2, transcendentals=0
        ),
    )(covariance)


def line_sum_kernel(size, partial_ref, out_ref, arriving, running, in_sem, up_sem, down_sem, fan_sem):
    me = lax.axis_index("elem")
    root = size // 2
    side = jnp.where(me < root, 0, 1)
    toward = jnp.where(me < root, me + 1, me - 1)
    outward = jnp.where(me < root, me - 1, me + 1)
    at_root = me == root
    at_end = (me == 0) | (me == size - 1)
    inner = jnp.logical_not(at_root | at_end)
    chunks = partial_ref.shape[0] // CHUNK

    barrier = pltpu.get_barrier_semaphore()

    @pl.when(me > 0)
    def _():
        pl.semaphore_signal(barrier, inc=1, device_id={"elem": me - 1}, device_id_type=MESH)

    @pl.when(me < size - 1)
    def _():
        pl.semaphore_signal(barrier, inc=1, device_id={"elem": me + 1}, device_id_type=MESH)

    @pl.when(at_end)
    def _():
        pl.semaphore_wait(barrier, 1)

    @pl.when(jnp.logical_not(at_end))
    def _():
        pl.semaphore_wait(barrier, 2)

    def rows(chunk):
        return pl.ds(pl.multiple_of(chunk * CHUNK, CHUNK), CHUNK)

    def inward(source, chunk):
        return pltpu.make_async_remote_copy(
            src_ref=source.at[rows(chunk)],
            dst_ref=arriving.at[side, rows(chunk)],
            send_sem=up_sem.at[chunk],
            recv_sem=in_sem.at[side, chunk],
            device_id={"elem": toward},
            device_id_type=MESH,
        )

    def arrival(which, chunk):
        return pltpu.make_async_remote_copy(
            src_ref=partial_ref.at[rows(chunk)],
            dst_ref=arriving.at[which, rows(chunk)],
            send_sem=up_sem.at[chunk],
            recv_sem=in_sem.at[which, chunk],
            device_id={"elem": toward},
            device_id_type=MESH,
        )

    def back(target, way, chunk):
        return pltpu.make_async_remote_copy(
            src_ref=out_ref.at[rows(chunk)],
            dst_ref=out_ref.at[rows(chunk)],
            send_sem=fan_sem.at[way, chunk],
            recv_sem=down_sem.at[chunk],
            device_id={"elem": target},
            device_id_type=MESH,
        )

    @pl.when(at_end)
    def _():
        @pl.loop(0, chunks)
        def _(chunk):
            inward(partial_ref, chunk).start()

        @pl.loop(0, chunks)
        def _(chunk):
            back(toward, 0, chunk).wait_recv()
            inward(partial_ref, chunk).wait_send()

    @pl.when(inner)
    def _():
        def pass_on(chunk):
            back(toward, 0, chunk).wait_recv()
            back(outward, 0, chunk).start()

        @pl.loop(0, chunks)
        def _(chunk):
            arrival(side, chunk).wait_recv()
            running[rows(chunk), :] = partial_ref[rows(chunk), :] + arriving[side, rows(chunk), :]
            inward(running, chunk).start()

            @pl.when(chunk >= LAG)
            def _():
                pass_on(chunk - LAG)

        @pl.loop(chunks - LAG, chunks)
        def _(chunk):
            pass_on(chunk)

        @pl.loop(0, chunks)
        def _(chunk):
            inward(running, chunk).wait_send()
            back(outward, 0, chunk).wait_send()

    @pl.when(at_root)
    def _():
        @pl.loop(0, chunks)
        def _(chunk):
            arrival(0, chunk).wait_recv()
            arrival(1, chunk).wait_recv()
            out_ref[rows(chunk), :] = partial_ref[rows(chunk), :] + (
                arriving[0, rows(chunk), :] + arriving[1, rows(chunk), :]
            )
            back(root - 1, 0, chunk).start()
            back(root + 1, 1, chunk).start()

        @pl.loop(0, chunks)
        def _(chunk):
            back(root - 1, 0, chunk).wait_send()
            back(root + 1, 1, chunk).wait_send()


def line_sum(partial):
    size = lax.axis_size("elem")
    row_count, width = partial.shape
    chunks = row_count // CHUNK
    return pl.pallas_call(
        functools.partial(line_sum_kernel, size),
        out_shape=jax.ShapeDtypeStruct(partial.shape, jnp.float32),
        in_specs=[pl.BlockSpec(memory_space=pltpu.VMEM)],
        out_specs=pl.BlockSpec(memory_space=pltpu.VMEM),
        scratch_shapes=[
            pltpu.VMEM((2, row_count, width), jnp.float32),
            pltpu.VMEM((row_count, width), jnp.float32),
            pltpu.SemaphoreType.DMA((2, chunks)),
            pltpu.SemaphoreType.DMA((chunks,)),
            pltpu.SemaphoreType.DMA((chunks,)),
            pltpu.SemaphoreType.DMA((2, chunks)),
        ],
        compiler_params=pltpu.CompilerParams(
            collective_id=0, has_side_effects=True, vmem_limit_bytes=32 * 1024 * 1024
        ),
    )(partial)


def local(samples, taps_weight, retain):
    row_count = samples.shape[0]
    elem_width = samples.shape[1]
    tap_count = taps_weight.shape[0]
    beam_count = taps_weight.shape[2]
    sample_history = shifted(samples[row_count - (tap_count - 1) :], "tm", 1)
    extended = jnp.concatenate([sample_history, samples], 0)
    windowed = jnp.concatenate(
        [
            extended[
                tap_count - 1 - filter_tap_index : tap_count - 1 - filter_tap_index + row_count
            ]
            for filter_tap_index in range(tap_count)
        ],
        1,
    )
    filters = taps_weight.reshape(tap_count * elem_width, beam_count)
    log_retain = jnp.log(retain)
    log_total = jnp.sum(log_retain)
    row_weight = jnp.exp(log_total - jnp.cumsum(log_retain))
    factor = jnp.exp(log_total)
    mass = jnp.sum(row_weight)
    groups = lax.axis_size("elem")
    mine = lax.axis_index("elem")
    blocks = lax.axis_size("tm")
    block = lax.axis_index("tm")
    columns = beam_count // groups
    beam_rows = line_sum(jnp.dot(windowed, filters, preferred_element_type=jnp.float32))
    weighted = beam_rows * row_weight[:, None]
    strips = [
        lax.dot_general(
            weighted[:, start : start + BLOCK],
            beam_rows[:, start:],
            (((0,), (0,)), ((), ())),
            precision=lax.Precision.HIGHEST,
        )
        for start in range(0, beam_count, BLOCK)
    ]
    packed = jnp.concatenate(strips, 1)
    width = packed.shape[1]
    scalars = jnp.concatenate([jnp.full((4, width), mass), jnp.full((4, width), factor)], 0)
    pieces = lax.all_gather(jnp.concatenate([packed, scalars], 0), "tm")
    total = jnp.zeros((BLOCK, width), jnp.float32)
    count = jnp.zeros((1, width), jnp.float32)
    for position in range(blocks):
        decay = pieces[position, BLOCK + 4 : BLOCK + 5]
        taken = position <= block
        total = jnp.where(taken, total * decay + pieces[position, :BLOCK], total)
        count = jnp.where(taken, count * decay + pieces[position, BLOCK : BLOCK + 1], count)
    estimate = total / count
    upper, at = [], 0
    for start in range(0, beam_count, BLOCK):
        strip = estimate[:, at : at + beam_count - start]
        at += beam_count - start
        upper.append(jnp.pad(strip, ((0, 0), (start, 0))))
    covariance = jnp.concatenate(upper, 0) + loading_level * jnp.eye(beam_count, dtype=jnp.float32)
    inverse_lower = inverse_factor(covariance)
    local_rows = lax.dynamic_slice_in_dim(inverse_lower, mine * columns, columns, 0)
    return lax.dot_general(
        local_rows, beam_rows, (((1,), (1,)), ((), ())), precision=lax.Precision.HIGHEST
    )


def solution(mesh):
    placed = (P("tm", "elem"), P(None, "elem", None), P("tm"))
    return jax.shard_map(
        local, mesh=mesh, in_specs=placed, out_specs=P("elem", "tm"), check_vma=False
    )
```
